32 devices in a mesh: rep: 2 (over x), pool: 8 (over z, y), tp: 2 (over core).
Axes of the slice: x: 2, y: 2, z: 4, core: 2. Of those that a mesh axis runs over, the one named last changes fastest.
Arguments:
- doc_hidden: bfloat16 [8192, 8192], P(('rep', 'pool'), 'tp'), parts along dimension 0, may hold values from -6 to 6
- key_projector: bfloat16 [8192, 1024], P(None, 'tp'), may hold values from -0.0625 to 0.0625
- value_projector: bfloat16 [8192, 1024], P(None, 'tp'), may hold values from -0.0625 to 0.0625
- queries: bfloat16 [256, 8192], P(('rep', 'pool'), 'tp'), parts along dimension 0, may hold values from -136 to 136
- lengths: int32 [256], P('rep'), parts along dimension 0, may hold values from 1024 to 4096, as said below
- page_slots: int32 [512], P('rep'), parts along dimension 0, may hold values from 0 to 255, as said below
- out_weight: bfloat16 [8192, 8192], P('tp', 'pool'), may hold values from -0.5 to 0.5
Outputs:
- kv_cache: bfloat16 [8192, 2, 1024], P(('rep', 'pool'), None, 'tp'), parts along dimension 0
- answer: bfloat16 [256, 8192], P('rep', ('pool', 'tp')), parts along dimension 0
The draws below stay inside these ranges and needn't reach their ends.
There are 2 independent parts, one for each index of `rep`. The reference program is written for one: setup_inputs(seed, part) draws one part's arguments, and reference() takes and returns one part's arrays. A program takes and returns all parts, laid end to end along the dimension named above; an argument that names none is the same for every part. Nothing has to cross between parts.
Inputs may be any that keep to these rules, and one draw needn't show every extreme that they name: `lengths`: each question row reads at least 1024 tokens; some row reads all 4096 and some row exactly 1024. `page_slots`: A permutation of the page numbers. Page p is made by pool index p // 32, and cache slot s belongs to pool index s // 32; at most 5 pages of one pool index go to one pool index, and that many do in every draw.
All inputs are finite; a program needn't handle non-finite values.
Results may differ from the reference program's by a relative error of at most 0.012.
The reference program's roundings to bfloat16 on the way count: a program that leaves them out, or rounds other values in their place, can miss the bound.
Values may be sent and summed in bfloat16 or wider, within the bound.
A program may use at most 128 MiB of HBM per device.

```python
import math
import jax
import jax.numpy as jnp
from jax import lax

MODEL_WIDTH = 8192
QUERY_HEAD_COUNT = 64
KEY_VALUE_HEADS = 8
HEAD_SIZE = 128
QUESTION_ROWS = 128
PAGE = 16
DOCUMENT_TOKENS = 4096
PAGES_DEV = 32
PAGES = 256
LMIN = 1024
N_POOL = 8


def draw_queries(key, part):
    key = jax.random.fold_in(key, 1)
    split_keys = jax.random.split(key, 1)
    entries = jax.random.normal(split_keys[0], (QUESTION_ROWS, QUERY_HEAD_COUNT * HEAD_SIZE), jnp.float32) * 2.0
    return jnp.clip(entries, -12.0, 12.0).astype(jnp.bfloat16)


def draw_lengths(key, part):
    key = jax.random.fold_in(key, 2)
    split_keys = jax.random.split(key, 3)
    drawn = jax.random.randint(split_keys[0], (QUESTION_ROWS,), LMIN, DOCUMENT_TOKENS + 1)
    longest = jax.random.randint(split_keys[1], (), 0, QUESTION_ROWS)
    shortest = (longest + 1 + jax.random.randint(split_keys[2], (), 0, QUESTION_ROWS - 1)) % QUESTION_ROWS
    drawn = drawn.at[longest].set(DOCUMENT_TOKENS).at[shortest].set(LMIN)
    return drawn.astype(jnp.int32)


def draw_page_slots(key, part):
    key = jax.random.fold_in(key, 3)
    split_keys = jax.random.split(key, 2)
    pool_count = N_POOL
    per_device = PAGES_DEV
    baseline = per_device // pool_count
    indices = jnp.arange(pool_count, dtype=jnp.int32)
    pairing = jax.random.permutation(split_keys[0], pool_count).astype(jnp.int32)
    shifted = jnp.roll(pairing, -1)
    counts = baseline + (indices[None, :] == pairing[:, None]).astype(jnp.int32) - (indices[None, :] == shifted[:, None]).astype(jnp.int32)

    def expand(row_counts):
        return jnp.repeat(indices, row_counts, total_repeat_length=per_device)
    targets = jax.vmap(expand)(counts)
    row_keys = jax.random.split(split_keys[1], pool_count)

    def shuffle(sub_key):
        return jax.random.permutation(sub_key, per_device).astype(jnp.int32)
    orders = jax.vmap(shuffle)(row_keys)
    targets = jnp.take_along_axis(targets, orders, axis=1)
    before = jnp.cumsum(counts, axis=0) - counts
    local_index = jnp.arange(per_device, dtype=jnp.int32)
    earlier = local_index[None, :] < local_index[:, None]
    ranking = jnp.sum(((targets[:, :, None] == targets[:, None, :]) & earlier[None, :, :]).astype(jnp.int32), axis=-1)
    slot_ids = targets * per_device + jnp.take_along_axis(before, targets, axis=1) + ranking
    return slot_ids.reshape(-1).astype(jnp.int32)


def levels(key, dims, cuts, smallest, high):
    gain, own = 1.0, jax.random.fold_in(key, 6)
    for axis_at, shards_of in cuts:
        heights = jnp.exp(jax.random.uniform(jax.random.fold_in(own, axis_at), (shards_of,), jnp.float32, smallest / len(cuts), high / len(cuts)))
        gain = gain * jnp.repeat(heights, dims[axis_at] // shards_of).reshape([-1 if axis == axis_at else 1 for axis in range(len(dims))])
    return gain


def centred(stream_key, shape, deviation, most, cuts=(), kind=jnp.bfloat16):
    values = deviation * jax.random.normal(stream_key, shape, jnp.float32)
    if cuts:
        values = values * levels(stream_key, shape, cuts, -0.22, 0.18)
    return jnp.clip(values, -most, most).astype(kind)


def setup_inputs(seed: int = 0, part: int = 0) -> dict:
    keys = jax.random.split(jax.random.key(seed), 8)
    part_keys = jax.random.split(jax.random.fold_in(keys[7], part), 8)
    doc_hidden = centred(part_keys[0], (DOCUMENT_TOKENS, MODEL_WIDTH), 1.0, 6.0, ((0, 8), (1, 2)))
    key_projector = centred(keys[1], (MODEL_WIDTH, KEY_VALUE_HEADS * HEAD_SIZE), MODEL_WIDTH ** -0.5, 0.0625, ((1, 2),))
    value_projector = centred(keys[2], (MODEL_WIDTH, KEY_VALUE_HEADS * HEAD_SIZE), MODEL_WIDTH ** -0.5, 0.0625, ((1, 2),))
    queries = draw_queries(jax.random.fold_in(jax.random.fold_in(keys[7], part), 71), part)
    lengths = draw_lengths(jax.random.fold_in(jax.random.fold_in(keys[7], part), 71), part)
    page_slots = draw_page_slots(jax.random.fold_in(jax.random.fold_in(keys[7], part), 71), part)
    out_weight = centred(keys[6], (QUERY_HEAD_COUNT * HEAD_SIZE, MODEL_WIDTH), HEAD_SIZE ** -0.5, 0.5, ((0, 2), (1, 8)))
    return {"doc_hidden": doc_hidden, "key_projector": key_projector, "value_projector": value_projector, "queries": queries, "lengths": lengths, "page_slots": page_slots, "out_weight": out_weight}


def reference(doc_hidden, key_projector, value_projector, queries, lengths, page_slots, out_weight):
    hidden = doc_hidden.astype(jnp.float32)
    normed = (hidden * lax.rsqrt(lax.optimization_barrier(jnp.mean(hidden * hidden, axis=-1, keepdims=True)) + 1e-06)).astype(jnp.bfloat16)
    document_key_rows = jnp.dot(normed, key_projector, preferred_element_type=jnp.float32).astype(jnp.bfloat16)
    document_value_rows = jnp.dot(normed, value_projector, preferred_element_type=jnp.float32).astype(jnp.bfloat16)
    page_of = jnp.zeros((PAGES,), jnp.int32).at[page_slots].set(jnp.arange(PAGES, dtype=jnp.int32))
    row_index = (page_of[:, None] * PAGE + jnp.arange(PAGE, dtype=jnp.int32)[None, :]).reshape(-1)
    stacked = jnp.stack([document_key_rows, document_value_rows], axis=1)
    kv_cache = stacked[row_index]
    query_group_width = QUERY_HEAD_COUNT // KEY_VALUE_HEADS
    inv_root = 1.0 / math.sqrt(HEAD_SIZE)
    query_single_float = queries.astype(jnp.float32).reshape(QUESTION_ROWS, KEY_VALUE_HEADS, query_group_width, HEAD_SIZE).transpose(1, 0, 2, 3)
    key_single_float = document_key_rows.astype(jnp.float32).reshape(DOCUMENT_TOKENS, KEY_VALUE_HEADS, HEAD_SIZE).transpose(1, 0, 2)
    value_single_float = document_value_rows.astype(jnp.float32).reshape(DOCUMENT_TOKENS, KEY_VALUE_HEADS, HEAD_SIZE).transpose(1, 0, 2)
    visible = jnp.arange(DOCUMENT_TOKENS, dtype=jnp.int32)[None, :] < lengths[:, None]

    def head_attention(operands):
        query_head, key_head, value_head = operands
        scores = jnp.einsum('qjd,td->qjt', query_head, key_head, precision=lax.Precision.HIGHEST) * inv_root
        masked = jnp.where(visible[:, None, :], scores, -1e+30)
        largest = lax.optimization_barrier(jnp.max(masked, axis=-1, keepdims=True))
        weights = jnp.where(visible[:, None, :], jnp.exp(scores - largest), 0.0)
        totals = lax.optimization_barrier(jnp.sum(weights, axis=-1))
        rounded = lax.optimization_barrier(weights.astype(jnp.bfloat16)).astype(jnp.float32)
        weighted = jnp.einsum('qjt,td->qjd', rounded, value_head, precision=lax.Precision.HIGHEST)
        return weighted / totals[..., None]
    heads_out = lax.map(head_attention, (query_single_float, key_single_float, value_single_float))
    attended = heads_out.transpose(1, 0, 2, 3).reshape(QUESTION_ROWS, QUERY_HEAD_COUNT * HEAD_SIZE).astype(jnp.bfloat16)
    answer = jnp.dot(attended, out_weight, preferred_element_type=jnp.float32).astype(jnp.bfloat16)
    return (kv_cache, answer)
```

```python
import functools
import math

import jax
import jax.numpy as jnp
from jax import lax
from jax.experimental import pallas as pl
from jax.experimental.pallas import tpu as pltpu
from jax.sharding import PartitionSpec as P

HEAD = 128
MESH = pl.DeviceIdType.MESH
F32 = jnp.float32
BF16 = jnp.bfloat16


def iota(shape, dim):
    return lax.broadcasted_iota(jnp.int32, shape, dim)


def kernel(
    n, rows, group, page, per, cap,
    doc, wk, wv, q, lens, slots, ow,
    kv_out, ans,
    x, w, wo, qall, kvb, vt, onehot_in, outb, recvb,
    ol, ml, own_o, own_ml, so, sst, ro, rst, att, amat, psend, precv,
    dsem, dsend, drecv, qsend, qrecv, asend, arecv, ksend, krecv,
    osend, orecv, tsend, trecv, psem,
):
    p = lax.axis_index("pool")
    t = lax.axis_index("tp")
    half = n // 2
    tokens = kvb.shape[0] * page
    heads = vt.shape[0]
    width = group * rows
    kvw = heads * HEAD
    snake = n == 8

    if snake:
        z = p // 2
        pos = z + (p % 2) * (n - 1 - 2 * z)
    else:
        pos = p

    def at(k):
        r = (pos + (k % n)) % n
        if not snake:
            return r
        h = r // half
        return 2 * r + h * (2 * (n - 1 - r) + 1 - 2 * r)

    other = 1 - t
    barrier = pltpu.get_barrier_semaphore()
    for k in range(1, n):
        pl.semaphore_signal(barrier, inc=1, device_id={"pool": at(k)}, device_id_type=MESH)
    pl.semaphore_signal(barrier, inc=1, device_id={"tp": other}, device_id_type=MESH)

    nb = dsend.shape[0]
    brows = tokens // nb
    blk = lambda b: pl.ds(b * brows, brows)
    dloc = [pltpu.make_async_copy(doc.at[blk(b)], x.at[t, blk(b)], dsem.at[b]) for b in range(nb)]
    for c in dloc:
        c.start()
    wc = [
        pltpu.make_async_copy(wk, w.at[:, pl.ds(0, kvw)], dsem.at[nb]),
        pltpu.make_async_copy(wv, w.at[:, pl.ds(kvw, kvw)], dsem.at[nb + 1]),
    ]
    oc = pltpu.make_async_copy(ow, wo, dsem.at[nb + 2])
    for c in wc:
        c.start()

    for g in range(heads):
        parts = [
            q[:, (group * g + j) * HEAD : (group * g + j + 1) * HEAD].astype(F32)
            for j in range(group)
        ]
        qall[p, g] = jnp.concatenate(parts, axis=0).astype(BF16)

    pl.semaphore_wait(barrier, n)

    dex = [
        pltpu.make_async_remote_copy(
            doc.at[blk(b)], x.at[t, blk(b)], dsend.at[b], drecv.at[b],
            device_id={"tp": other}, device_id_type=MESH,
        )
        for b in range(nb)
    ]
    for c in dex:
        c.start()
    oc.start()

    def ring(buf, ssem, rsem, s):
        hh = heads // 2
        a, b = at(-s), at(s)
        if s == half - 1:
            ra, rb = buf.at[a, pl.ds(0, hh)], buf.at[b, pl.ds(hh, heads - hh)]
        else:
            ra, rb = buf.at[a], buf.at[b]
        return (
            pltpu.make_async_remote_copy(
                ra, ra, ssem.at[0, s], rsem.at[0, s],
                device_id={"pool": at(1)}, device_id_type=MESH,
            ),
            pltpu.make_async_remote_copy(
                rb, rb, ssem.at[1, s], rsem.at[1, s],
                device_id={"pool": at(-1)}, device_id_type=MESH,
            ),
        )

    def advance(steps, s):
        if s > 0:
            for c in steps[s - 1]:
                c.wait_recv()
        if s < half:
            for c in steps[s]:
                c.start()

    qring = [ring(qall, qsend, qrecv, s) for s in range(half)]
    advance(qring, 0)

    total = n * per
    shift = per.bit_length() - 1
    srow = jnp.broadcast_to(slots[...], (total, total))
    ir, ic = iota((total, total), 0), iota((total, total), 1)
    scol = jnp.sum(jnp.where(ir == ic, srow, 0).astype(F32), axis=1, keepdims=True).astype(jnp.int32)
    tr, tc = srow >> shift, jnp.broadcast_to(scol >> shift, (total, total))
    same = (tr == tc) & ((ir >> shift) == (ic >> shift)) & (ir < ic)
    rank = jnp.sum(jnp.where(same, 1.0, 0.0), axis=0, keepdims=True)
    pageid = iota((1, total), 1)
    dest = (slots[...] >> shift).astype(F32) * cap + rank
    spread = jnp.where(
        iota((total, tokens), 0) == p * per + iota((total, tokens), 1) // page, 1.0, 0.0
    ).astype(BF16)
    dtok = jnp.dot(
        jnp.broadcast_to(dest, (16, total)).astype(BF16), spread, preferred_element_type=F32
    )[0:1].astype(jnp.int32)
    drow = dtok * page + iota((1, tokens), 1) % page
    origin = (pageid >> shift).astype(F32) * cap + rank
    hit = jnp.broadcast_to(slots[...], (tokens, total)) == p * per + iota((tokens, total), 0) // page
    rpage = jnp.sum(
        jnp.where(hit, jnp.broadcast_to(origin, (tokens, total)), 0.0), axis=1, keepdims=True
    ).astype(jnp.int32)
    rrow = rpage * page + iota((tokens, 1), 0) % page
    moved = n * cap * page
    onehot_in[...] = jnp.where(iota((tokens, moved), 1) == rrow, 1.0, 0.0).astype(BF16)

    feat = x.shape[2]
    cols = 256
    qstep = 1
    for b in range(nb):
        dloc[b].wait()
        dex[b].wait_recv()

        @pl.loop(0, brows // 16)
        def _(i):
            r = pl.ds(pl.multiple_of(b * brows + i * 16, 16), 16)
            ss = jnp.zeros((16, 1), F32)
            for h in range(2):
                v = x[h, r, :].astype(F32)
                ss = ss + jnp.sum(v * v, axis=-1, keepdims=True)
            scale = lax.rsqrt(ss / (2 * feat) + 1e-06)
            for h in range(2):
                x[h, r, :] = (x[h, r, :].astype(F32) * scale).astype(BF16)

        if qstep < half:
            advance(qring, qstep)
            qstep += 1
        if b == 0:
            for c in wc:
                c.wait()

        @pl.loop(0, 2 * kvw // cols)
        def _(i):
            cc = pl.ds(pl.multiple_of(i * cols, cols), cols)
            acc = jnp.dot(x[0, blk(b), :], w[pl.ds(0, feat), cc], preferred_element_type=F32)
            acc += jnp.dot(x[1, blk(b), :], w[pl.ds(feat, feat), cc], preferred_element_type=F32)
            kvb[pl.ds(b * brows // page, brows // page), :, cc] = acc.astype(BF16).reshape(
                brows // page, page, cols
            )

        if qstep < half:
            advance(qring, qstep)
            qstep += 1

    onehot_out = jnp.where(iota((moved, tokens), 0) == drow, 1.0, 0.0).astype(BF16)

    @pl.loop(0, 2 * kvw // cols)
    def _(i):
        cc = pl.ds(pl.multiple_of(i * cols, cols), cols)
        outb[:, :, cc] = (
            jnp.dot(onehot_out, kvb[:, :, cc].reshape(tokens, cols), preferred_element_type=F32)
            .astype(BF16)
            .reshape(n, cap * page, cols)
        )

    recvb[p] = outb[p]
    ksends = [
        pltpu.make_async_remote_copy(
            outb.at[at(k)], recvb.at[p], ksend.at[k - 1], krecv.at[k - 1],
            device_id={"pool": at(k)}, device_id_type=MESH,
        )
        for k in range(1, n)
    ]
    ksends[0].start()

    while qstep <= half:
        advance(qring, qstep)
        qstep += 1

    for g in range(heads):
        vt[g] = (
            kvb[:, :, kvw + g * HEAD : kvw + (g + 1) * HEAD]
            .reshape(tokens, HEAD).astype(F32).T.astype(BF16)
        )

    lr = jnp.broadcast_to(lens[...], (n * rows, n * rows))
    eye = iota((n * rows, n * rows), 0) == iota((n * rows, n * rows), 1)
    lcol = jnp.sum(jnp.where(eye, lr, 0).astype(F32), axis=1, keepdims=True)

    def chunk_lengths(c):
        want = c * rows + iota((n * rows, width), 1) % rows
        pick = jnp.where(iota((n * rows, width), 0) == want, jnp.broadcast_to(lcol, (n * rows, width)), 0.0)
        return jnp.sum(pick, axis=0, keepdims=True).astype(jnp.int32)

    inv_root = 1.0 / math.sqrt(HEAD)

    def attend(ca, cb):
        lim = jnp.concatenate([chunk_lengths(ca), chunk_lengths(cb)], axis=1)
        seen = p * tokens + iota((tokens, 2 * width), 0) < lim

        @pl.loop(0, heads)
        def _(g):
            qq = jnp.concatenate([qall[ca, g], qall[cb, g]], axis=0)
            kk = kvb[:, :, pl.ds(pl.multiple_of(g * HEAD, HEAD), HEAD)].reshape(tokens, HEAD)
            sc = lax.dot_general(kk, qq, (((1,), (1,)), ((), ())), preferred_element_type=F32) * inv_root
            sc = jnp.where(seen, sc, -1e30)
            m = jnp.max(sc, axis=0, keepdims=True)
            e = jnp.where(seen, jnp.exp(sc - m), 0.0)
            ml[g, 0:1, :] = m
            ml[g, 1:2, :] = jnp.sum(e, axis=0, keepdims=True)
            ol[g] = jnp.dot(vt[g], e.astype(BF16), preferred_element_type=F32)

    def merge(parts):
        top = functools.reduce(jnp.maximum, [m for m, _, _ in parts])
        e = [jnp.exp(m - top) for m, _, _ in parts]
        l = sum(a * b for a, (_, b, _) in zip(e, parts))
        o = sum(a * b for a, (_, _, b) in zip(e, parts))
        return top, l, o

    def held(side, g):
        c = slice(side * width, (side + 1) * width)
        return ml[g, 0:1, c], ml[g, 1:2, c], ol[g, :, c]

    def came(side, s, g):
        return rst[side, s, g, 0:1, :], rst[side, s, g, 1:2, :], ro[side, s, g].astype(F32)

    hh = heads // 2
    halves = (range(0, hh), range(hh, heads))
    osteps = []
    for s in range(half):
        d = half - s
        attend(at(d), p if s == 0 else at(-d))
        if s == 0:
            for g in range(heads):
                m, l, o = held(1, g)
                own_ml[g, 0:1, :] = m
                own_ml[g, 1:2, :] = l
                own_o[g] = o
        else:
            for c in osteps[s - 1]:
                c.wait_recv()
        step = []
        for side in range(2):
            todo = halves[side] if s == 0 else range(heads)
            for g in todo:
                parts = [held(0 if s == 0 else side, g)]
                if s > 1 or (s == 1 and g in halves[side]):
                    parts.append(came(side, s - 1, g))
                m, l, o = merge(parts) if len(parts) > 1 else parts[0]
                sst[side, s, g, 0:1, :] = m
                sst[side, s, g, 1:2, :] = l
                so[side, s, g] = o.astype(BF16)
            sel = pl.ds(todo[0], len(todo))
            for src, dst, a, b in ((so, ro, osend, orecv), (sst, rst, tsend, trecv)):
                step.append(
                    pltpu.make_async_remote_copy(
                        src.at[side, s, sel], dst.at[side, s, sel], a.at[side, s], b.at[side, s],
                        device_id={"pool": at(1 - 2 * side)}, device_id_type=MESH,
                    )
                )
        for c in step:
            c.start()
        osteps.append(step)
        if s + 1 < n - 1:
            ksends[s + 1].start()
    for c in osteps[half - 1]:
        c.wait_recv()
    for g in range(heads):
        parts = [
            (own_ml[g, 0:1, :], own_ml[g, 1:2, :], own_o[g]),
            came(0, half - 1, g),
            came(1, half - 1, g),
        ]
        _, l, o = merge(parts)
        att[p, g] = (o / l).T.astype(BF16)

    aring = [ring(att, asend, arecv, s) for s in range(half)]
    for s in range(half + 1):
        advance(aring, s)
        if s < half and half + s + 1 < n - 1:
            ksends[half + s + 1].start()

    for g in range(heads):
        planes = [att[c, g].astype(F32) for c in range(n)]
        for j in range(group):
            amat[:, (g * group + j) * HEAD : (g * group + j + 1) * HEAD] = jnp.concatenate(
                [v[j * rows : (j + 1) * rows] for v in planes], axis=0
            ).astype(BF16)
    oc.wait()
    oh = wo.shape[1] // 2

    def project(which, dst):
        @pl.loop(0, oh // cols)
        def _(i):
            src = pl.ds(pl.multiple_of(which * oh + i * cols, cols), cols)
            dst[:, pl.ds(pl.multiple_of(i * cols, cols), cols)] = jnp.dot(
                amat[...], wo[:, src], preferred_element_type=F32
            )

    project(other, psend)
    pcopy = pltpu.make_async_remote_copy(
        psend, precv, psem.at[0], psem.at[1], device_id={"tp": other}, device_id_type=MESH
    )
    pcopy.start()
    mine = [
        jnp.dot(
            amat[...],
            wo[:, pl.ds(pl.multiple_of(t * oh + i * cols, cols), cols)],
            preferred_element_type=F32,
        )
        for i in range(oh // cols)
    ]
    pcopy.wait_recv()
    for i, v in enumerate(mine):
        cc = slice(i * cols, (i + 1) * cols)
        ans[:, cc] = (v + precv[:, cc]).astype(BF16)

    for c in ksends:
        c.wait_recv()

    @pl.loop(0, 2 * kvw // cols)
    def _(i):
        cc = pl.ds(pl.multiple_of(i * cols, cols), cols)
        kv_out[:, cc] = jnp.dot(
            onehot_in[...], recvb[:, :, cc].reshape(moved, cols), preferred_element_type=F32
        ).astype(BF16)

    for c in dex + ksends + [pcopy]:
        c.wait_send()
    for s in range(half):
        for c in (*qring[s], *osteps[s], *aring[s]):
            c.wait_send()


def shards(doc_hidden, key_projector, value_projector, queries, lengths, page_slots, out_weight):
    n = lax.axis_size("pool")
    tokens, feat = doc_hidden.shape
    kvw = key_projector.shape[1]
    heads = kvw // HEAD
    rows = queries.shape[0]
    group = queries.shape[1] // kvw
    per = page_slots.shape[0] // n
    page = tokens // per
    cap = per // n + 1
    width = group * rows
    half = n // 2
    nb = 2
    oc = out_weight.shape[1]
    moved = cap * page
    any_spec = pl.BlockSpec(memory_space=pl.ANY)
    vmem = pl.BlockSpec(memory_space=pltpu.VMEM)
    dma = pltpu.SemaphoreType.DMA
    kv, ans = pl.pallas_call(
        functools.partial(kernel, n, rows, group, page, per, cap),
        out_shape=(
            jax.ShapeDtypeStruct((tokens, 2 * kvw), BF16),
            jax.ShapeDtypeStruct((n * rows, oc // 2), BF16),
        ),
        in_specs=[any_spec, any_spec, any_spec, vmem, vmem, vmem, any_spec],
        out_specs=(vmem, vmem),
        scratch_shapes=[
            pltpu.VMEM((2, tokens, feat), BF16),
            pltpu.VMEM((2 * feat, 2 * kvw), BF16),
            pltpu.VMEM(out_weight.shape, BF16),
            pltpu.VMEM((n, heads, width, HEAD), BF16),
            pltpu.VMEM((per, page, 2 * kvw), BF16),
            pltpu.VMEM((heads, HEAD, tokens), BF16),
            pltpu.VMEM((tokens, n * moved), BF16),
            pltpu.VMEM((n, moved, 2 * kvw), BF16),
            pltpu.VMEM((n, moved, 2 * kvw), BF16),
            pltpu.VMEM((heads, HEAD, 2 * width), F32),
            pltpu.VMEM((heads, 8, 2 * width), F32),
            pltpu.VMEM((heads, HEAD, width), F32),
            pltpu.VMEM((heads, 8, width), F32),
            pltpu.VMEM((2, half, heads, HEAD, width), BF16),
            pltpu.VMEM((2, half, heads, 8, width), F32),
            pltpu.VMEM((2, half, heads, HEAD, width), BF16),
            pltpu.VMEM((2, half, heads, 8, width), F32),
            pltpu.VMEM((n, heads, width, HEAD), BF16),
            pltpu.VMEM((n * rows, out_weight.shape[0]), BF16),
            pltpu.VMEM((n * rows, oc // 2), F32),
            pltpu.VMEM((n * rows, oc // 2), F32),
            dma((nb + 3,)), dma((nb,)), dma((nb,)),
            dma((2, half)), dma((2, half)), dma((2, half)), dma((2, half)),
            dma((n - 1,)), dma((n - 1,)),
            dma((2, half)), dma((2, half)), dma((2, half)), dma((2, half)),
            dma((2,)),
        ],
        compiler_params=pltpu.CompilerParams(
            collective_id=0, has_side_effects=True, vmem_limit_bytes=60 * 1024 * 1024
        ),
    )(
        doc_hidden, key_projector, value_projector, queries,
        lengths.reshape(1, -1), page_slots.reshape(1, -1), out_weight,
    )
    return kv.reshape(tokens, 2, kvw), ans


def solution(mesh):
    in_specs = (
        P(("rep", "pool"), "tp"),
        P(None, "tp"),
        P(None, "tp"),
        P(("rep", "pool"), "tp"),
        P("rep"),
        P("rep"),
        P("tp", "pool"),
    )
    out_specs = (P(("rep", "pool"), None, "tp"), P("rep", ("pool", "tp")))
    return jax.shard_map(shards, mesh=mesh, in_specs=in_specs, out_specs=out_specs, check_vma=False)
```

```python
import functools
import math

import jax
import jax.numpy as jnp
from jax import lax
from jax.experimental import pallas as pl
from jax.experimental.pallas import tpu as pltpu
from jax.sharding import PartitionSpec as P

HEAD = 128
MESH = pl.DeviceIdType.MESH
F32 = jnp.float32
BF16 = jnp.bfloat16


def iota(shape, dim):
    return lax.broadcasted_iota(jnp.int32, shape, dim)


def kernel(
    n, rows, group, page, per, cap,
    doc, wk, wv, q, lens, slots, ow,
    kv_out, ans,
    x, w, wo, qall, kvb, vt, onehot_in, outb, recvb,
    ol, ml, own_o, own_ml, so, sst, ro, rst, att, amat, psend, precv,
    dsem, dsend, drecv, qsend, qrecv, asend, arecv, ksend, krecv,
    osend, orecv, tsend, trecv, psem,
):
    p = lax.axis_index("pool")
    t = lax.axis_index("tp")
    half = n // 2
    tokens = kvb.shape[0] * page
    heads = vt.shape[0]
    width = group * rows
    kvw = heads * HEAD
    snake = n == 8

    if snake:
        z = p // 2
        pos = z + (p % 2) * (n - 1 - 2 * z)
    else:
        pos = p

    def at(k):
        r = (pos + (k % n)) % n
        if not snake:
            return r
        h = r // half
        return 2 * r + h * (2 * (n - 1 - r) + 1 - 2 * r)

    other = 1 - t
    barrier = pltpu.get_barrier_semaphore()
    for k in range(1, n):
        pl.semaphore_signal(barrier, inc=1, device_id={"pool": at(k)}, device_id_type=MESH)
    pl.semaphore_signal(barrier, inc=1, device_id={"tp": other}, device_id_type=MESH)

    nb = dsend.shape[0]
    brows = tokens // nb
    blk = lambda b: pl.ds(b * brows, brows)
    dloc = [pltpu.make_async_copy(doc.at[blk(b)], x.at[t, blk(b)], dsem.at[b]) for b in range(nb)]
    for c in dloc:
        c.start()
    wc = [
        pltpu.make_async_copy(wk, w.at[:, pl.ds(0, kvw)], dsem.at[nb]),
        pltpu.make_async_copy(wv, w.at[:, pl.ds(kvw, kvw)], dsem.at[nb + 1]),
    ]
    oc = pltpu.make_async_copy(ow, wo, dsem.at[nb + 2])
    for c in wc:
        c.start()

    for g in range(heads):
        parts = [
            q[:, (group * g + j) * HEAD : (group * g + j + 1) * HEAD].astype(F32)
            for j in range(group)
        ]
        qall[p, g] = jnp.concatenate(parts, axis=0).astype(BF16)

    pl.semaphore_wait(barrier, n)

    dex = [
        pltpu.make_async_remote_copy(
            doc.at[blk(b)], x.at[t, blk(b)], dsend.at[b], drecv.at[b],
            device_id={"tp": other}, device_id_type=MESH,
        )
        for b in range(nb)
    ]
    for c in dex:
        c.start()

    hh = heads // 2
    halves = (range(0, hh), range(hh, heads))

    def ring(buf, ssem, rsem, s):
        return {
            (side, g): pltpu.make_async_remote_copy(
                buf.at[at(s * (2 * side - 1)), g], buf.at[at(s * (2 * side - 1)), g],
                ssem.at[side, s, g], rsem.at[side, s, g],
                device_id={"pool": at(1 - 2 * side)}, device_id_type=MESH,
            )
            for g in range(heads)
            for side in range(2)
            if s < half - 1 or g in halves[side]
        }

    def order(side, g):
        return (g, side) if side == 0 else (heads - 1 - g, side)

    def advance(steps, s):
        keys = sorted(steps[min(s, half - 1)] if s == 0 else steps[s - 1], key=lambda k: order(*k))
        for k in keys:
            if s > 0:
                steps[s - 1][k].wait_recv()
            if s < half and k in steps[s]:
                steps[s][k].start()

    qring = [ring(qall, qsend, qrecv, s) for s in range(half)]
    advance(qring, 0)

    total = n * per
    shift = per.bit_length() - 1
    srow = jnp.broadcast_to(slots[...], (total, total))
    ir, ic = iota((total, total), 0), iota((total, total), 1)
    scol = jnp.sum(jnp.where(ir == ic, srow, 0).astype(F32), axis=1, keepdims=True).astype(jnp.int32)
    tr, tc = srow >> shift, jnp.broadcast_to(scol >> shift, (total, total))
    same = (tr == tc) & ((ir >> shift) == (ic >> shift)) & (ir < ic)
    rank = jnp.sum(jnp.where(same, 1.0, 0.0), axis=0, keepdims=True)
    pageid = iota((1, total), 1)
    dest = (slots[...] >> shift).astype(F32) * cap + rank
    spread = jnp.where(
        iota((total, tokens), 0) == p * per + iota((total, tokens), 1) // page, 1.0, 0.0
    ).astype(BF16)
    dtok = jnp.dot(
        jnp.broadcast_to(dest, (16, total)).astype(BF16), spread, preferred_element_type=F32
    )[0:1].astype(jnp.int32)
    drow = dtok * page + iota((1, tokens), 1) % page
    origin = (pageid >> shift).astype(F32) * cap + rank
    hit = jnp.broadcast_to(slots[...], (tokens, total)) == p * per + iota((tokens, total), 0) // page
    rpage = jnp.sum(
        jnp.where(hit, jnp.broadcast_to(origin, (tokens, total)), 0.0), axis=1, keepdims=True
    ).astype(jnp.int32)
    rrow = rpage * page + iota((tokens, 1), 0) % page
    moved = n * cap * page
    onehot_in[...] = jnp.where(iota((tokens, moved), 1) == rrow, 1.0, 0.0).astype(BF16)

    feat = x.shape[2]
    cols = 256
    nsub = 2 * kvw // cols

    def norm(r):
        ss = jnp.zeros((16, 1), F32)
        for h in range(2):
            v = x[h, r, :].astype(F32)
            ss = ss + jnp.sum(v * v, axis=-1, keepdims=True)
        scale = lax.rsqrt(ss / (2 * feat) + 1e-06)
        for h in range(2):
            x[h, r, :] = (x[h, r, :].astype(F32) * scale).astype(BF16)

    def multiply(b, i):
        cc = pl.ds(pl.multiple_of(i * cols, cols), cols)
        acc = jnp.dot(x[0, blk(b), :], w[pl.ds(0, feat), cc], preferred_element_type=F32)
        acc += jnp.dot(x[1, blk(b), :], w[pl.ds(feat, feat), cc], preferred_element_type=F32)
        kvb[pl.ds(b * brows // page, brows // page), :, cc] = acc.astype(BF16).reshape(
            brows // page, page, cols
        )

    dloc[0].wait()
    dex[0].wait_recv()

    @pl.loop(0, brows // 16)
    def _(i):
        norm(pl.ds(pl.multiple_of(i * 16, 16), 16))

    advance(qring, 1)
    wc[0].wait()
    dloc[1].wait()
    dex[1].wait_recv()
    each = brows // 16 // (kvw // cols)

    @pl.loop(0, kvw // cols)
    def _(i):
        multiply(0, i)
        for e in range(each):
            norm(pl.ds(pl.multiple_of(brows + (i * each + e) * 16, 16), 16))

    wc[1].wait()
    oc.start()
    qstep = 2
    if half >= qstep:
        advance(qring, qstep)
        qstep += 1

    @pl.loop(0, kvw // cols)
    def _(i):
        multiply(1, i)

    if half >= qstep:
        advance(qring, qstep)
        qstep += 1

    @pl.loop(kvw // cols, nsub)
    def _(i):
        multiply(0, i)
        multiply(1, i)

    onehot_out = jnp.where(iota((moved, tokens), 0) == drow, 1.0, 0.0).astype(BF16)

    @pl.loop(0, 2 * kvw // cols)
    def _(i):
        cc = pl.ds(pl.multiple_of(i * cols, cols), cols)
        outb[:, :, cc] = (
            jnp.dot(onehot_out, kvb[:, :, cc].reshape(tokens, cols), preferred_element_type=F32)
            .astype(BF16)
            .reshape(n, cap * page, cols)
        )

    recvb[p] = outb[p]
    ksends = [
        pltpu.make_async_remote_copy(
            outb.at[at(k)], recvb.at[p], ksend.at[k - 1], krecv.at[k - 1],
            device_id={"pool": at(k)}, device_id_type=MESH,
        )
        for k in range(1, n)
    ]

    def kv_start(step):
        turns = {0: (0, n - 2), half: (1, n - 3), 2 * half: range(2, n - 3)}
        for i in turns.get(step, ()):
            ksends[i].start()

    kv_start(0)

    while qstep <= half:
        advance(qring, qstep)
        qstep += 1

    for g in range(heads):
        vt[g] = (
            kvb[:, :, kvw + g * HEAD : kvw + (g + 1) * HEAD]
            .reshape(tokens, HEAD).astype(F32).T.astype(BF16)
        )

    lr = jnp.broadcast_to(lens[...], (n * rows, n * rows))
    eye = iota((n * rows, n * rows), 0) == iota((n * rows, n * rows), 1)
    lcol = jnp.sum(jnp.where(eye, lr, 0).astype(F32), axis=1, keepdims=True)

    def chunk_lengths(c):
        want = c * rows + iota((n * rows, width), 1) % rows
        pick = jnp.where(iota((n * rows, width), 0) == want, jnp.broadcast_to(lcol, (n * rows, width)), 0.0)
        return jnp.sum(pick, axis=0, keepdims=True).astype(jnp.int32)

    inv_root = 1.0 / math.sqrt(HEAD)

    def attend(ca, cb):
        lim = jnp.concatenate([chunk_lengths(ca), chunk_lengths(cb)], axis=1)
        seen = p * tokens + iota((tokens, 2 * width), 0) < lim

        @pl.loop(0, heads)
        def _(g):
            qq = jnp.concatenate([qall[ca, g], qall[cb, g]], axis=0)
            kk = kvb[:, :, pl.ds(pl.multiple_of(g * HEAD, HEAD), HEAD)].reshape(tokens, HEAD)
            sc = lax.dot_general(kk, qq, (((1,), (1,)), ((), ())), preferred_element_type=F32) * inv_root
            sc = jnp.where(seen, sc, -1e30)
            m = jnp.max(sc, axis=0, keepdims=True)
            e = jnp.where(seen, jnp.exp(sc - m), 0.0)
            ml[g, 0:1, :] = m
            ml[g, 1:2, :] = jnp.sum(e, axis=0, keepdims=True)
            ol[g] = jnp.dot(vt[g], e.astype(BF16), preferred_element_type=F32)

    def held(side, g):
        c = slice(side * width, (side + 1) * width)
        return ml[g, 0:1, c], ml[g, 1:2, c], ol[g, :, c]

    def stats(side, s, g):
        return rst[side, s, g : g + 1, :], rst[side, s, heads + g : heads + g + 1, :]

    osteps = []
    for s in range(half):
        d = half - s
        attend(at(d), p if s == 0 else at(-d))
        if s == 0:
            for g in range(heads):
                m, l, o = held(1, g)
                own_ml[g : g + 1, :] = m
                own_ml[heads + g : heads + g + 1, :] = l
                own_o[g] = o
        step = {}
        for side in range(2):
            to = dict(device_id={"pool": at(1 - 2 * side)}, device_id_type=MESH)
            step[side, -1] = pltpu.make_async_remote_copy(
                sst.at[side, s], rst.at[side, s], tsend.at[side, s], trecv.at[side, s], **to
            )
            for g in range(heads):
                if s > 0 or g in halves[side]:
                    step[side, g] = pltpu.make_async_remote_copy(
                        so.at[side, s, g], ro.at[side, s, g],
                        osend.at[side, s, g], orecv.at[side, s, g], **to
                    )
        if s > 0:
            for side in range(2):
                osteps[s - 1][side, -1].wait_recv()
        for side in range(2):
            for g in range(heads):
                m, l, _ = held(0 if s == 0 else side, g)
                if s > 1 or (s == 1 and g in halves[side]):
                    m1, l1 = stats(side, s - 1, g)
                    top = jnp.maximum(m, m1)
                    l = l * jnp.exp(m - top) + l1 * jnp.exp(m1 - top)
                    m = top
                sst[side, s, g : g + 1, :] = m
                sst[side, s, heads + g : heads + g + 1, :] = l
            step[side, -1].start()
        for side, g in sorted(
            (k for k in step if k[1] >= 0), key=lambda k: (k[1] in halves[k[0]], order(*k))
        ):
            m, l, o = held(0 if s == 0 else side, g)
            if s > 1 or (s == 1 and g in halves[side]):
                osteps[s - 1][side, g].wait_recv()
                m1, l1 = stats(side, s - 1, g)
                top = jnp.maximum(m, m1)
                o = o * jnp.exp(m - top) + ro[side, s - 1, g].astype(F32) * jnp.exp(m1 - top)
            so[side, s, g] = o.astype(BF16)
            step[side, g].start()
        osteps.append(step)
        kv_start(s + 1)
    for side in range(2):
        osteps[half - 1][side, -1].wait_recv()
    aring = [ring(att, asend, arecv, s) for s in range(half)]
    for g in range(heads):
        ms = [own_ml[g : g + 1, :]]
        ls = [own_ml[heads + g : heads + g + 1, :]]
        os = [own_o[g]]
        for side in range(2):
            osteps[half - 1][side, g].wait_recv()
            m1, l1 = stats(side, half - 1, g)
            ms.append(m1)
            ls.append(l1)
            os.append(ro[side, half - 1, g].astype(F32))
        top = functools.reduce(jnp.maximum, ms)
        e = [jnp.exp(m - top) for m in ms]
        l = sum(a * b for a, b in zip(e, ls))
        o = sum(a * b for a, b in zip(e, os))
        att[p, g] = (o / l).T.astype(BF16)
        for side in range(2):
            if (side, g) in aring[0]:
                aring[0][side, g].start()
    kv_start(half + 1)
    for s in range(1, half + 1):
        advance(aring, s)
        kv_start(half + s + 1)

    for g in range(heads):
        planes = [att[c, g].astype(F32) for c in range(n)]
        for j in range(group):
            amat[:, (g * group + j) * HEAD : (g * group + j + 1) * HEAD] = jnp.concatenate(
                [v[j * rows : (j + 1) * rows] for v in planes], axis=0
            ).astype(BF16)
    oc.wait()
    oh = wo.shape[1] // 2

    def project(which, dst):
        @pl.loop(0, oh // cols)
        def _(i):
            src = pl.ds(pl.multiple_of(which * oh + i * cols, cols), cols)
            dst[:, pl.ds(pl.multiple_of(i * cols, cols), cols)] = jnp.dot(
                amat[...], wo[:, src], preferred_element_type=F32
            )

    project(other, psend)
    pcopy = pltpu.make_async_remote_copy(
        psend, precv, psem.at[0], psem.at[1], device_id={"tp": other}, device_id_type=MESH
    )
    pcopy.start()
    mine = [
        jnp.dot(
            amat[...],
            wo[:, pl.ds(pl.multiple_of(t * oh + i * cols, cols), cols)],
            preferred_element_type=F32,
        )
        for i in range(oh // cols)
    ]
    pcopy.wait_recv()
    for i, v in enumerate(mine):
        cc = slice(i * cols, (i + 1) * cols)
        ans[:, cc] = (v + precv[:, cc]).astype(BF16)

    for c in ksends:
        c.wait_recv()

    @pl.loop(0, 2 * kvw // cols)
    def _(i):
        cc = pl.ds(pl.multiple_of(i * cols, cols), cols)
        kv_out[:, cc] = jnp.dot(
            onehot_in[...], recvb[:, :, cc].reshape(moved, cols), preferred_element_type=F32
        ).astype(BF16)

    for c in dex + ksends + [pcopy]:
        c.wait_send()
    for s in range(half):
        for c in (*qring[s].values(), *osteps[s].values(), *aring[s].values()):
            c.wait_send()


def shards(doc_hidden, key_projector, value_projector, queries, lengths, page_slots, out_weight):
    n = lax.axis_size("pool")
    tokens, feat = doc_hidden.shape
    kvw = key_projector.shape[1]
    heads = kvw // HEAD
    rows = queries.shape[0]
    group = queries.shape[1] // kvw
    per = page_slots.shape[0] // n
    page = tokens // per
    cap = per // n + 1
    width = group * rows
    half = n // 2
    nb = 2
    oc = out_weight.shape[1]
    moved = cap * page
    any_spec = pl.BlockSpec(memory_space=pl.ANY)
    vmem = pl.BlockSpec(memory_space=pltpu.VMEM)
    dma = pltpu.SemaphoreType.DMA
    kv, ans = pl.pallas_call(
        functools.partial(kernel, n, rows, group, page, per, cap),
        out_shape=(
            jax.ShapeDtypeStruct((tokens, 2 * kvw), BF16),
            jax.ShapeDtypeStruct((n * rows, oc // 2), BF16),
        ),
        in_specs=[any_spec, any_spec, any_spec, vmem, vmem, vmem, any_spec],
        out_specs=(vmem, vmem),
        scratch_shapes=[
            pltpu.VMEM((2, tokens, feat), BF16),
            pltpu.VMEM((2 * feat, 2 * kvw), BF16),
            pltpu.VMEM(out_weight.shape, BF16),
            pltpu.VMEM((n, heads, width, HEAD), BF16),
            pltpu.VMEM((per, page, 2 * kvw), BF16),
            pltpu.VMEM((heads, HEAD, tokens), BF16),
            pltpu.VMEM((tokens, n * moved), BF16),
            pltpu.VMEM((n, moved, 2 * kvw), BF16),
            pltpu.VMEM((n, moved, 2 * kvw), BF16),
            pltpu.VMEM((heads, HEAD, 2 * width), F32),
            pltpu.VMEM((heads, 8, 2 * width), F32),
            pltpu.VMEM((heads, HEAD, width), F32),
            pltpu.VMEM((2 * heads, width), F32),
            pltpu.VMEM((2, half, heads, HEAD, width), BF16),
            pltpu.VMEM((2, half, 2 * heads, width), F32),
            pltpu.VMEM((2, half, heads, HEAD, width), BF16),
            pltpu.VMEM((2, half, 2 * heads, width), F32),
            pltpu.VMEM((n, heads, width, HEAD), BF16),
            pltpu.VMEM((n * rows, out_weight.shape[0]), BF16),
            pltpu.VMEM((n * rows, oc // 2), F32),
            pltpu.VMEM((n * rows, oc // 2), F32),
            dma((nb + 3,)), dma((nb,)), dma((nb,)),
            dma((2, half, heads)), dma((2, half, heads)),
            dma((2, half, heads)), dma((2, half, heads)),
            dma((n - 1,)), dma((n - 1,)),
            dma((2, half, heads)), dma((2, half, heads)), dma((2, half)), dma((2, half)),
            dma((2,)),
        ],
        compiler_params=pltpu.CompilerParams(
            collective_id=0, has_side_effects=True, vmem_limit_bytes=60 * 1024 * 1024
        ),
    )(
        doc_hidden, key_projector, value_projector, queries,
        lengths.reshape(1, -1), page_slots.reshape(1, -1), out_weight,
    )
    return kv.reshape(tokens, 2, kvw), ans


def solution(mesh):
    in_specs = (
        P(("rep", "pool"), "tp"),
        P(None, "tp"),
        P(None, "tp"),
        P(("rep", "pool"), "tp"),
        P("rep"),
        P("rep"),
        P("tp", "pool"),
    )
    out_specs = (P(("rep", "pool"), None, "tp"), P("rep", ("pool", "tp")))
    return jax.shard_map(shards, mesh=mesh, in_specs=in_specs, out_specs=out_specs, check_vma=False)
```
